128 devices in a mesh: lat: 16 (over z, y_hi, core), lon: 8 (over y_lo, x).
Axes of the slice: x: 4, y: 4 (y_hi: 2, y_lo: 2; y = y_hi * 2 + y_lo), z: 4, core: 2. Of those that a mesh axis runs over, the one named last changes fastest.
Arguments:
- tokens: bfloat16 [8, 96, 576, 192], P(None, 'lat', 'lon'), may hold values from -6 to 6
- bias_table: float32 [16, 4, 6, 3312], P('lat'), may hold values from -4 to 243
- index_table: int32 [144, 144], replicated, may hold values from 0 to 3311
- gain_attn: float32 [192], replicated, may hold values from 0.1 to 1.9
- w_qkv: bfloat16 [192, 576], replicated, may hold values from -0.4375 to 0.4375
- w_proj: bfloat16 [192, 192], replicated, may hold values from -0.4375 to 0.4375
- gain_mlp: float32 [192], replicated, may hold values from 0.1 to 1.9
- w_up: bfloat16 [192, 768], replicated, may hold values from -0.4375 to 0.4375
- w_down: bfloat16 [768, 192], replicated, may hold values from -0.21875 to 0.21875
Outputs:
- block_out: bfloat16 [8, 96, 576, 192], P(None, 'lat', 'lon')
The draws below stay inside these ranges and needn't reach their ends.
All inputs are finite; a program needn't handle non-finite values.
Results may differ from the reference program's by a relative error of at most 0.013.
Values may be sent and summed in bfloat16 or wider, within the bound.
No kernel may reach another device: no remote copies, remote signals or barrier semaphores. Data moves between devices by JAX's collectives and lax.ppermute only.
A program may use at most 320 MiB of HBM per device.

```python
from functools import partial
import jax
import jax.numpy as jnp
from jax import lax

C = 192
HEADS = 6
FFH = 768
HD = 32
ZL = 8
WZ = 2
WLAT = 6
WLON = 12
WIN = 144
POS = 3312
ZW = 4
NLAT = 96
NLON = 576
LATW = 16


def draw_bias_table(key, part):
    key = jax.random.fold_in(key, 11)
    normal_key = jax.random.fold_in(key, 0)
    table_shape = (LATW, ZW, HEADS, POS)
    table_values = jnp.clip(jax.random.normal(normal_key, table_shape, jnp.float32), -4.0, 4.0)
    return table_values.astype(jnp.float32)


def plant(values, stream_key, smallest, high):
    longest = values.shape.index(max(values.shape))
    spots = []
    for shift in (0, 1):
        where = [jax.random.randint(jax.random.fold_in(stream_key, axis), (), 0, length) for axis, length in enumerate(values.shape)]
        where[longest] = (where[longest] + shift) % values.shape[longest]
        spots.append(tuple(where))
    return values.at[spots[0]].set(smallest).at[spots[1]].set(high)


def levels(key, shape, cuts, smallest, high):
    level, own = 1.0, jax.random.fold_in(key, 6)
    for position, shards_of in cuts:
        steps = jnp.exp(jax.random.uniform(jax.random.fold_in(own, position), (shards_of,), jnp.float32, smallest / len(cuts), high / len(cuts)))
        level = level * jnp.repeat(steps, shape[position] // shards_of).reshape([-1 if axis == position else 1 for axis in range(len(shape))])
    return level


def normal_values(key, shape, spread, most, shards=(), kind=jnp.bfloat16):
    loudness = levels(key, shape, shards, -0.22, 0.18) if shards else 1.0
    values = jax.random.normal(key, shape, jnp.float32) * spread * loudness
    return jnp.minimum(jnp.maximum(values, -most), most).astype(kind)


def setup_inputs(seed: int = 0) -> dict:
    key_of = jax.random.split(jax.random.key(seed), 10)
    return {
        "tokens": normal_values(key_of[0], (ZL, NLAT, NLON, C), 1.0, 6.0, ((1, 16), (2, 8))),
        "bias_table": draw_bias_table(jax.random.fold_in(key_of[9], 71), 0),
        "index_table": plant(jax.random.randint(key_of[2], (WIN, WIN), 0, POS), jax.random.fold_in(key_of[2], 1), 0, POS - 1).astype(jnp.int32),
        "gain_attn": jnp.clip(1.0 + 0.18 * jax.random.normal(key_of[3], (C,), jnp.float32), 0.1, 1.9),
        "w_qkv": normal_values(key_of[4], (C, 3 * C), C ** -0.5, 0.4375),
        "w_proj": normal_values(key_of[5], (C, C), C ** -0.5, 0.4375),
        "gain_mlp": jnp.clip(1.0 + 0.18 * jax.random.normal(key_of[6], (C,), jnp.float32), 0.1, 1.9),
        "w_up": normal_values(key_of[7], (C, FFH), C ** -0.5, 0.4375),
        "w_down": normal_values(key_of[8], (FFH, C), FFH ** -0.5, 0.21875),
    }


epsilon = 1e-05

def normalize(values, gain):
    average = lax.optimization_barrier(jnp.mean(values, axis=-1, keepdims=True))
    centered = values - average
    variance = lax.optimization_barrier(jnp.mean(centered * centered, axis=-1, keepdims=True))
    return centered * lax.rsqrt(variance + epsilon) * gain.astype(jnp.float32)

def window_row(inputs, index_table, gain_attn, w_qkv, w_proj):
    row_slab, row_codes, row_bias = inputs
    lon_windows = NLON // WLON
    normed = normalize(row_slab.astype(jnp.float32), gain_attn).astype(jnp.bfloat16)
    windows = normed.reshape(WZ, WLAT, lon_windows, WLON, C).transpose(2, 0, 1, 3, 4).reshape(lon_windows * WIN, C)
    packed = jnp.dot(windows, w_qkv, preferred_element_type=jnp.float32).astype(jnp.bfloat16)
    packed = packed.reshape(lon_windows, WIN, 3, HEADS, HD)
    queries = packed[:, :, 0].astype(jnp.float32)
    keys_all = packed[:, :, 1].astype(jnp.float32)
    values_all = packed[:, :, 2].astype(jnp.float32)
    scores = jnp.einsum('wqhd,wkhd->whqk', queries, keys_all) * HD ** (-0.5)
    pair_bias = jnp.take(row_bias, index_table, axis=1)
    scores = scores + pair_bias[None]
    labels = row_codes.reshape(WLAT, lon_windows, WLON).transpose(1, 0, 2).reshape(lon_windows, WLAT * WLON)
    labels = jnp.tile(labels, (1, WZ))
    allowed = labels[:, :, None] == labels[:, None, :]
    scores = jnp.where(allowed[:, None], scores, -1e+30)
    attn_probs = jax.nn.softmax(scores, axis=-1).astype(jnp.bfloat16)
    head_out = jnp.einsum('whqk,wkhd->wqhd', attn_probs.astype(jnp.float32), values_all)
    head_out = head_out.astype(jnp.bfloat16).reshape(lon_windows * WIN, C)
    projected = jnp.dot(head_out, w_proj, preferred_element_type=jnp.float32)
    return projected.reshape(lon_windows, WZ, WLAT, WLON, C).transpose(1, 2, 0, 3, 4).reshape(WZ, WLAT, NLON, C)

def feed_forward(summed, gain_mlp, w_up, w_down):
    normed = normalize(summed, gain_mlp).astype(jnp.bfloat16)
    hidden = jax.nn.gelu(jnp.dot(normed, w_up, preferred_element_type=jnp.float32), approximate=False)
    hidden = hidden.astype(jnp.bfloat16)
    return (summed + jnp.dot(hidden, w_down, preferred_element_type=jnp.float32)).astype(jnp.bfloat16)

def reference(tokens, bias_table, index_table, gain_attn, w_qkv, w_proj, gain_mlp, w_up, w_down):
    half_lat = WLAT // 2
    half_lon = WLON // 2
    orig_rows = (jnp.arange(NLAT, dtype=jnp.int32) + half_lat) % NLAT
    flags = (orig_rows >= NLAT - half_lat).astype(jnp.int32)
    codes = jnp.broadcast_to(flags[:, None], (NLAT, NLON))
    code_rows = codes.reshape(LATW, WLAT, NLON)
    row_step = partial(window_row, index_table=index_table, gain_attn=gain_attn, w_qkv=w_qkv, w_proj=w_proj)
    mlp_step = partial(feed_forward, gain_mlp=gain_mlp, w_up=w_up, w_down=w_down)

    def level_group(inputs):
        group_slab, group_bias = inputs
        shifted = jnp.roll(group_slab, (-half_lat, -half_lon), axis=(1, 2))
        row_slabs = shifted.reshape(WZ, LATW, WLAT, NLON, C).transpose(1, 0, 2, 3, 4)
        attn_rows = lax.map(row_step, (row_slabs, code_rows, group_bias))
        attn_shifted = attn_rows.transpose(1, 0, 2, 3, 4).reshape(WZ, NLAT, NLON, C)
        attn = jnp.roll(attn_shifted, (half_lat, half_lon), axis=(1, 2))
        resid = group_slab.astype(jnp.float32) + attn
        mixed = lax.map(mlp_step, resid.reshape(WZ * NLAT, NLON, C))
        return mixed.reshape(WZ, NLAT, NLON, C)
    groups = tokens.reshape(ZW, WZ, NLAT, NLON, C)
    result = lax.map(level_group, (groups, bias_table.transpose(1, 0, 2, 3)))
    return result.reshape(ZL, NLAT, NLON, C)
```

```python
import jax
import jax.numpy as jnp
import numpy as np
from jax import lax
from jax.experimental import pallas as pl
from jax.experimental.pallas import tpu as pltpu
from jax.sharding import PartitionSpec as P

HEADS = 6
HD = 32
C = 192
FFH = 768
ZW = 4
COLS = 72
UNITS = 12
WINS = 7
SLOT = 40
NEG = -1e30
LOG2E = 1.4426950408889634
EPS = 1e-05
F32 = jnp.float32
BF16 = jnp.bfloat16
GELU = (0.7978822019334538, 0.03634471964715062, -4.492210425823531e-05,
        -5.034912992251254e-05, 3.0967343436505324e-06, -6.630250880453595e-08)


def head_row(h):
    return h * SLOT + (8 if h >= 3 else 0)


def unit_place(c):
    return (c + 1) // 2, (c + 1) % 2


def gather_maps():
    perm = np.zeros((504, 432), np.float32)
    left = np.zeros((72, 48), np.float32)
    right = np.zeros((72, 48), np.float32)
    back = np.zeros((432, 480), np.float32)
    for c in range(-1, 13):
        m, half = unit_place(c)
        for r in range(6):
            for j in range(6):
                row = 72 * m + 36 * half + r * 6 + j
                if c == -1:
                    left[row, r * 8 + 2 + j] = 1
                elif c == 12:
                    right[row - 432, r * 8 + j] = 1
                else:
                    perm[row, r * COLS + 6 * c + j] = 1
                    back[r * COLS + 6 * c + j, c * SLOT + 4 * half + r * 6 + j] = 1
    return [x.astype(jnp.bfloat16) for x in (perm, left, right, back)]


def key_position(latw, key):
    halo, rest = divmod(key, 72)
    half, rest = divmod(rest, 36)
    dz, rest = divmod(rest, 18)
    di, j = divmod(rest, 6)
    upper = (latw == 0) == (halo == 0)
    return (dz * 6 + di + (3 if upper else 0)) * 12 + 6 * half + j


def index_maps():
    keys = np.zeros((2, 3, 48, 144), np.float32)
    lanes = np.zeros((2, 2, 3, 144, 128), np.float32)
    for latw in range(2):
        for key in range(144):
            keys[latw, key // 48, key % 48, key_position(latw, key)] = 1
        for half in range(2):
            for s in range(36):
                pos = key_position(latw, 36 * half + s)
                for third in range(3):
                    lanes[latw, half, third, pos, third * SLOT + 4 * half + s] = 1
    return keys.astype(jnp.bfloat16), lanes.astype(jnp.bfloat16)


def nt(a, b):
    return lax.dot_general(a, b, (((1,), (1,)), ((), ())), preferred_element_type=F32)


def tn(a, b):
    return lax.dot_general(a, b, (((0,), (0,)), ((), ())), preferred_element_type=F32)


def nn(a, b):
    return jnp.dot(a, b, preferred_element_type=F32)


POS = 3312
CH = 13


def bias_kernel(cut_ref, table_ref, index_ref, keys_ref, lanes_ref, out_ref, thi, tlo, lo_s, hi_s, g_s):
    for ch in range(CH):
        width = min(256, POS - 256 * ch)
        rows = jnp.concatenate([table_ref[0, z, :, 256 * ch : 256 * ch + width] for z in range(ZW)], axis=0)
        if width < 256:
            rows = jnp.concatenate([rows, jnp.zeros((24, 256 - width), F32)], axis=1)
        rows = rows * LOG2E
        top = rows.astype(BF16).astype(F32)
        thi[24 * ch : 24 * ch + 24] = top
        tlo[24 * ch : 24 * ch + 24] = rows - top
    index = index_ref[...]
    index_lo = (index & 255).astype(F32).astype(BF16)
    index_hi = (index >> 8).astype(F32).astype(BF16)
    for half in range(2):
        for part, dst in ((index_lo, lo_s), (index_hi, hi_s)):
            total = jnp.zeros((48, 128), F32)
            for third in range(3):
                rows = nt(keys_ref[third], part).astype(BF16)
                total = total + nn(rows, lanes_ref[half, third])
            dst[48 * half : 48 * half + 48] = total.astype(jnp.int32)
    top = thi[...].astype(BF16)
    low = tlo[...].astype(BF16)
    both = jnp.concatenate([top, low], axis=1)
    spread = lax.broadcasted_iota(jnp.int32, (256, 128), 0)

    def step(i, _):
        lo = lo_s[pl.ds(i, 1), :]
        hi = hi_s[pl.ds(i, 1), :]
        lo2 = lo_s[pl.ds(i + 48, 1), :]
        hi2 = hi_s[pl.ds(i + 48, 1), :]
        hot = jnp.concatenate(
            [(spread == lo).astype(F32).astype(BF16), (spread == lo2).astype(F32).astype(BF16)], axis=1
        )
        vals = nn(top, hot) + nn(low, hot)
        his = jnp.concatenate([hi, hi2], axis=1)
        his = jnp.broadcast_to(his, (24, 256))
        acc = vals[0:24]
        for ch in range(1, CH):
            acc = jnp.where(his == ch, vals[24 * ch : 24 * ch + 24], acc)
        g_s[i] = acc
        return 0

    lax.fori_loop(0, 48, step, 0, unroll=2)
    lane = lax.broadcasted_iota(jnp.int32, (8, 128), 1)
    cut = cut_ref[0] == 1
    sub = lax.broadcasted_iota(jnp.int32, (144, 1), 0)

    def arrange(z, _):
        for half in range(2):
            for tile in range(2):
                for k8 in range(6):
                    three = [
                        g_s[pl.ds(8 * k8, 8), z * HEADS + 3 * tile + h, 128 * half : 128 * half + 128]
                        for h in range(3)
                    ]
                    for third in range(3):
                        moved = [
                            three[h] if h == third else pltpu.roll(three[h], (SLOT * (h - third)) % 128, 1)
                            for h in range(3)
                        ]
                        got = jnp.where(lane < SLOT, moved[0], jnp.where(lane < 2 * SLOT, moved[1], moved[2]))
                        row = 48 * third + 8 * k8
                        if row >= 72:
                            got = jnp.where(cut, NEG, got)
                        out_ref[z, half, row : row + 8, 128 * tile : 128 * tile + 128] = got
        return 0

    for z in range(ZW):
        arrange(z, 0)


def make_bias(cut, table, index_table, keys, lanes):
    return pl.pallas_call(
        bias_kernel,
        out_shape=jax.ShapeDtypeStruct((ZW, 2, 144, 256), F32),
        in_specs=[pl.BlockSpec(memory_space=pltpu.SMEM)] + [pl.BlockSpec(memory_space=pltpu.VMEM)] * 4,
        out_specs=pl.BlockSpec(memory_space=pltpu.VMEM),
        scratch_shapes=[
            pltpu.VMEM((24 * CH, 256), F32),
            pltpu.VMEM((24 * CH, 256), F32),
            pltpu.VMEM((96, 128), jnp.int32),
            pltpu.VMEM((96, 128), jnp.int32),
            pltpu.VMEM((48, 24, 256), F32),
        ],
        compiler_params=pltpu.CompilerParams(vmem_limit_bytes=48 * 2**20),
    )(cut, table, index_table, keys, lanes)


def block_kernel(own_ref, prev_ref, next_ref, lo_ref, lh_ref, ro_ref, rh_ref, bias0_ref, bias1_ref,
                 ga_ref, wqkv_ref, wproj_ref, gm_ref, wup_ref, wdown_ref,
                 perm_ref, left_ref, right_ref, back_ref, out_ref,
                 xs, ns, qs, kvs, os_, rs):
    latw = pl.program_id(1)
    first = latw == 0

    def flat(v):
        return v.astype(F32).reshape(-1, C).astype(BF16)

    own = flat(own_ref[...])
    halo = flat(jnp.where(first, prev_ref[...].astype(F32), next_ref[...].astype(F32)))
    perm = perm_ref[...]
    for base, block, l_ref, r_ref in ((0, own, lo_ref, ro_ref), (72, halo, lh_ref, rh_ref)):
        got = nn(perm, block)
        edge_l = nn(left_ref[...], flat(l_ref[...]))
        edge_r = nn(right_ref[...], flat(r_ref[...]))
        for m in range(WINS):
            piece = got[72 * m : 72 * m + 72]
            if m == 0:
                piece = piece + edge_l
            if m == WINS - 1:
                piece = piece + edge_r
            xs[144 * m + base : 144 * m + base + 72] = piece
    ones = jnp.ones((C, 128), BF16)
    gain = ga_ref[...]

    def both(v):
        return jnp.concatenate([v, v[:, : C - 128]], axis=1)

    for m in range(WINS):
        x = xs[144 * m : 144 * m + 144]
        mean = both(nn(x.astype(BF16), ones) * (1.0 / C))
        cen = x - mean
        var = nn((cen * cen).astype(BF16), ones) * (1.0 / C)
        inv = both(lax.rsqrt(var + EPS))
        ns[144 * m : 144 * m + 144] = (cen * inv * gain).astype(BF16)
    packed = nn(ns[...], wqkv_ref[...])
    qs[...] = packed[:, :C] * (HD ** -0.5 * LOG2E)
    kvs[...] = packed[:, C:].astype(BF16)
    lane = lax.broadcasted_iota(jnp.int32, (SLOT, C), 1) // HD
    for c in range(UNITS):
        m, half = unit_place(c)
        q = qs[144 * m + 32 * half : 144 * m + 32 * half + SLOT]
        pad = jnp.zeros((8, C), F32)
        rows = []
        for h in range(HEADS):
            rows.append(jnp.where(lane == h, q, 0.0))
            if h in (2, 5):
                rows.append(pad)
        qm = jnp.concatenate(rows, axis=0).astype(BF16)
        k = kvs[144 * m : 144 * m + 144, :C]
        v = kvs[144 * m : 144 * m + 144, C:]
        bias = jnp.where(first, bias0_ref[0, half], bias1_ref[0, half])
        s = nt(k, qm) + bias
        e = jnp.exp2(s - jnp.max(s, axis=0, keepdims=True))
        p = (e * (1.0 / jnp.sum(e, axis=0, keepdims=True))).astype(BF16)
        o = tn(p, v)
        out = o[0:SLOT]
        for h in range(1, HEADS):
            out = jnp.where(lane == h, o[head_row(h) : head_row(h) + SLOT], out)
        os_[SLOT * c : SLOT * c + SLOT] = out
        rs[SLOT * c : SLOT * c + SLOT] = xs[144 * m + 32 * half : 144 * m + 32 * half + SLOT]
    resid = rs[...] + nn(os_[...].astype(BF16), wproj_ref[...])
    mean = jnp.mean(resid, axis=1, keepdims=True)
    cen = resid - mean
    var = nn((cen * cen).astype(BF16), ones) * (1.0 / C)
    normed = (cen * both(lax.rsqrt(var + EPS)) * gm_ref[...]).astype(BF16)
    u = nn(normed, wup_ref[...])
    w = jnp.minimum(u * u, 25.0)
    poly = jnp.full_like(w, GELU[-1])
    for coef in GELU[-2::-1]:
        poly = poly * w + coef
    hu = 0.5 * u
    hidden = (hu + hu * jnp.tanh(u * poly)).astype(BF16)
    out = (resid + nn(hidden, wdown_ref[...])).astype(BF16)
    out_ref[...] = nn(back_ref[...], out).reshape(2, 3, COLS, C).astype(BF16)


def run_block(tokens, prev, nxt, left, right, bias0, bias1, ga, wqkv, wproj, gm, wup, wdown, maps):
    perm, lmap, rmap, back = maps
    whole = lambda shape: pl.BlockSpec(shape, lambda z, w: (0,) * len(shape))
    rows3 = (2, 3, COLS, C)
    edge = (2, 3, 8, C)
    return pl.pallas_call(
        block_kernel,
        grid=(ZW, 2),
        out_shape=jax.ShapeDtypeStruct(tokens.shape, BF16),
        in_specs=[
            pl.BlockSpec(rows3, lambda z, w: (z, w, 0, 0)),
            pl.BlockSpec(rows3, lambda z, w: (z, 0, 0, 0)),
            pl.BlockSpec(rows3, lambda z, w: (z, 0, 0, 0)),
            pl.BlockSpec(edge, lambda z, w: (z, 1 + w, 0, 0)),
            pl.BlockSpec(edge, lambda z, w: (z, 3 * w, 0, 0)),
            pl.BlockSpec(edge, lambda z, w: (z, 1 + w, 0, 0)),
            pl.BlockSpec(edge, lambda z, w: (z, 3 * w, 0, 0)),
            pl.BlockSpec((1, 2, 144, 256), lambda z, w: (z, 0, 0, 0)),
            pl.BlockSpec((1, 2, 144, 256), lambda z, w: (z, 0, 0, 0)),
            whole((1, C)), whole((C, 3 * C)), whole((C, C)), whole((1, C)), whole((C, FFH)), whole((FFH, C)),
            whole((504, 432)), whole((72, 48)), whole((72, 48)), whole((432, 480)),
        ],
        out_specs=pl.BlockSpec(rows3, lambda z, w: (z, w, 0, 0)),
        scratch_shapes=[
            pltpu.VMEM((1008, C), F32),
            pltpu.VMEM((1008, C), BF16),
            pltpu.VMEM((1008, C), F32),
            pltpu.VMEM((1008, 2 * C), BF16),
            pltpu.VMEM((480, C), F32),
            pltpu.VMEM((480, C), F32),
        ],
        compiler_params=pltpu.CompilerParams(vmem_limit_bytes=56 * 2**20),
    )(tokens, prev, nxt, left, left, right, right, bias0, bias1, ga, wqkv, wproj, gm, wup, wdown,
      perm, lmap, rmap, back)


def passed_along(block, axis, distance):
    count = lax.axis_size(axis)
    return lax.ppermute(block, axis, [((i - distance) % count, i) for i in range(count)])


def shards(tokens, bias_table, index_table, gain_attn, w_qkv, w_proj, gain_mlp, w_up, w_down):
    place = lax.axis_index("lat")
    last = lax.axis_size("lat") - 1
    prev_table = passed_along(bias_table, "lat", 1)
    prev = passed_along(tokens[:, 3:], "lat", 1)
    nxt = passed_along(tokens[:, :3], "lat", -1)
    rim_l = jnp.concatenate([prev[:, :, :8], tokens[:, :, :8], nxt[:, :, :8]], axis=1)
    rim_r = jnp.concatenate([prev[:, :, -8:], tokens[:, :, -8:], nxt[:, :, -8:]], axis=1)
    right = passed_along(rim_l, "lon", -1)
    left = passed_along(rim_r, "lon", 1)
    keys, lanes = index_maps()
    maps = gather_maps()
    cut1 = (place == last).astype(jnp.int32).reshape(1)
    cut0 = (place == 0).astype(jnp.int32).reshape(1)
    bias1 = make_bias(cut1, bias_table, index_table, keys[1], lanes[1])
    bias0 = make_bias(cut0, prev_table, index_table, keys[0], lanes[0])
    return run_block(tokens, prev, nxt, left, right, bias0, bias1,
                     gain_attn.reshape(1, C), w_qkv, w_proj, gain_mlp.reshape(1, C), w_up, w_down, maps)


def solution(mesh):
    return jax.shard_map(
        shards,
        mesh=mesh,
        in_specs=(
            P(None, "lat", "lon", None),
            P("lat", None, None, None),
            P(),
            P(),
            P(),
            P(),
            P(),
            P(),
            P(),
        ),
        out_specs=P(None, "lat", "lon", None),
        check_vma=False,
    )
```

```python
import jax
import jax.numpy as jnp
import numpy as np
from jax import lax
from jax.experimental import pallas as pl
from jax.experimental.pallas import tpu as pltpu
from jax.sharding import PartitionSpec as P

HEADS = 6
HD = 32
C = 192
FFH = 768
ZW = 4
COLS = 72
UNITS = 12
WINS = 7
SLOT = 40
NEG = -1e30
LOG2E = 1.4426950408889634
EPS = 1e-05
F32 = jnp.float32
BF16 = jnp.bfloat16
GELU = (0.7978822019334538, 0.03634471964715062, -4.492210425823531e-05,
        -5.034912992251254e-05, 3.0967343436505324e-06, -6.630250880453595e-08)


def head_row(h):
    return h * SLOT + (8 if h >= 3 else 0)


def unit_place(c):
    return (c + 1) // 2, (c + 1) % 2


def gather_maps():
    perm = np.zeros((504, 432), np.float32)
    left = np.zeros((72, 48), np.float32)
    right = np.zeros((72, 48), np.float32)
    back = np.zeros((432, 480), np.float32)
    for c in range(-1, 13):
        m, half = unit_place(c)
        for r in range(6):
            for j in range(6):
                row = 72 * m + 36 * half + r * 6 + j
                if c == -1:
                    left[row, r * 8 + 2 + j] = 1
                elif c == 12:
                    right[row - 432, r * 8 + j] = 1
                else:
                    perm[row, r * COLS + 6 * c + j] = 1
                    back[r * COLS + 6 * c + j, c * SLOT + 4 * half + r * 6 + j] = 1
    return [x.astype(jnp.bfloat16) for x in (perm, left, right, back)]


def key_position(latw, key):
    halo, rest = divmod(key, 72)
    half, rest = divmod(rest, 36)
    dz, rest = divmod(rest, 18)
    di, j = divmod(rest, 6)
    upper = (latw == 0) == (halo == 0)
    return (dz * 6 + di + (3 if upper else 0)) * 12 + 6 * half + j


def index_maps():
    keys = np.zeros((2, 3, 48, 144), np.float32)
    lanes = np.zeros((2, 2, 3, 144, 128), np.float32)
    for latw in range(2):
        for key in range(144):
            keys[latw, key // 48, key % 48, key_position(latw, key)] = 1
        for half in range(2):
            for s in range(36):
                pos = key_position(latw, 36 * half + s)
                for third in range(3):
                    lanes[latw, half, third, pos, third * SLOT + 4 * half + s] = 1
    return keys.astype(jnp.bfloat16), lanes.astype(jnp.bfloat16)


def nt(a, b):
    return lax.dot_general(a, b, (((1,), (1,)), ((), ())), preferred_element_type=F32)


def tn(a, b):
    return lax.dot_general(a, b, (((0,), (0,)), ((), ())), preferred_element_type=F32)


def nn(a, b):
    return jnp.dot(a, b, preferred_element_type=F32)


POS = 3312
CH = 13


def bias_kernel(cut_ref, table_ref, index_ref, keys_ref, lanes_ref, out_ref, thi, tlo, lo_s, hi_s, g_s):
    for ch in range(CH):
        width = min(256, POS - 256 * ch)
        rows = jnp.concatenate([table_ref[0, z, :, 256 * ch : 256 * ch + width] for z in range(ZW)], axis=0)
        if width < 256:
            rows = jnp.concatenate([rows, jnp.zeros((24, 256 - width), F32)], axis=1)
        rows = rows * LOG2E
        top = rows.astype(BF16).astype(F32)
        thi[24 * ch : 24 * ch + 24] = top
        tlo[24 * ch : 24 * ch + 24] = rows - top
    index = index_ref[...]
    index_lo = (index & 255).astype(F32).astype(BF16)
    index_hi = (index >> 8).astype(F32).astype(BF16)
    for half in range(2):
        for part, dst in ((index_lo, lo_s), (index_hi, hi_s)):
            total = jnp.zeros((48, 128), F32)
            for third in range(3):
                rows = nt(keys_ref[third], part).astype(BF16)
                total = total + nn(rows, lanes_ref[half, third])
            dst[48 * half : 48 * half + 48] = total.astype(jnp.int32)
    top = thi[...].astype(BF16)
    low = tlo[...].astype(BF16)
    both = jnp.concatenate([top, low], axis=0)
    spread = lax.broadcasted_iota(jnp.int32, (256, 128), 0).astype(F32).astype(BF16)

    def step(i, _):
        lo = lo_s[pl.ds(i, 1), :]
        hi = hi_s[pl.ds(i, 1), :]
        lo2 = lo_s[pl.ds(i + 48, 1), :]
        hi2 = hi_s[pl.ds(i + 48, 1), :]
        hot = jnp.concatenate(
            [jnp.where(spread == v.astype(F32).astype(BF16), BF16(1), BF16(0)) for v in (lo, lo2)], axis=1
        )
        vals = nn(both, hot)
        vals = vals[: 24 * CH] + vals[24 * CH :]
        his = jnp.concatenate([hi, hi2], axis=1)
        his = jnp.broadcast_to(his, (24, 256))
        acc = vals[0:24]
        for ch in range(1, CH):
            acc = jnp.where(his == ch, vals[24 * ch : 24 * ch + 24], acc)
        g_s[i] = acc
        return 0

    lax.fori_loop(0, 48, step, 0, unroll=8)
    lane = lax.broadcasted_iota(jnp.int32, (8, 128), 1)
    cut = cut_ref[0] == 1
    sub = lax.broadcasted_iota(jnp.int32, (144, 1), 0)

    def arrange(z, _):
        for half in range(2):
            for tile in range(2):
                for k8 in range(6):
                    three = [
                        g_s[pl.ds(8 * k8, 8), z * HEADS + 3 * tile + h, 128 * half : 128 * half + 128]
                        for h in range(3)
                    ]
                    for third in range(3):
                        moved = [
                            three[h] if h == third else pltpu.roll(three[h], (SLOT * (h - third)) % 128, 1)
                            for h in range(3)
                        ]
                        got = jnp.where(lane < SLOT, moved[0], jnp.where(lane < 2 * SLOT, moved[1], moved[2]))
                        row = 48 * third + 8 * k8
                        if row >= 72:
                            got = jnp.where(cut, NEG, got)
                        out_ref[z, half, row : row + 8, 128 * tile : 128 * tile + 128] = got
        return 0

    for z in range(ZW):
        arrange(z, 0)


def make_bias(cut, table, index_table, keys, lanes):
    return pl.pallas_call(
        bias_kernel,
        out_shape=jax.ShapeDtypeStruct((ZW, 2, 144, 256), F32),
        in_specs=[pl.BlockSpec(memory_space=pltpu.SMEM)] + [pl.BlockSpec(memory_space=pltpu.VMEM)] * 4,
        out_specs=pl.BlockSpec(memory_space=pltpu.VMEM),
        scratch_shapes=[
            pltpu.VMEM((24 * CH, 256), F32),
            pltpu.VMEM((24 * CH, 256), F32),
            pltpu.VMEM((96, 128), jnp.int32),
            pltpu.VMEM((96, 128), jnp.int32),
            pltpu.VMEM((48, 24, 256), F32),
        ],
        compiler_params=pltpu.CompilerParams(vmem_limit_bytes=16 * 2**20),
        cost_estimate=pl.CostEstimate(flops=8 * 10**9, bytes_accessed=2 * 10**6, transcendentals=0),
    )(cut, table, index_table, keys, lanes)


def packed_shape(levels, rows, cols):
    return jax.ShapeDtypeStruct((3 * levels // 2, rows, cols, 128), BF16)


def pack(dst, x):
    levels = x.shape[0]
    dst[:levels] = x[..., :128]
    for i in range(levels // 2):
        dst[levels + i] = jnp.concatenate([x[2 * i, ..., 128:], x[2 * i + 1, ..., 128:]], axis=-1)


def unpack(src, levels, z):
    low = src[pl.ds(2 * z, 2)].astype(F32)
    high = src[pl.ds(levels + z, 1)].astype(F32)
    rows = low.shape[1] * low.shape[2]
    low = low.reshape(2, rows, 128)
    high = high.reshape(rows, 128)
    parts = [jnp.concatenate([low[dz], high[:, 64 * dz : 64 * dz + 64]], axis=1) for dz in range(2)]
    return jnp.concatenate(parts, axis=0).astype(BF16)


def pack_kernel(x_ref, up, dn, er, el):
    pack(up, x_ref[:, 3:6])
    pack(dn, x_ref[:, 0:3])
    pack(er, x_ref[:, :, COLS - 8 :])
    pack(el, x_ref[:, :, :8])


def make_packs(tokens):
    vmem = pl.BlockSpec(memory_space=pltpu.VMEM)
    shapes = [packed_shape(8, 3, COLS)] * 2 + [packed_shape(8, 6, 8)] * 2
    return pl.pallas_call(
        pack_kernel,
        out_shape=shapes,
        in_specs=[vmem],
        out_specs=[vmem] * len(shapes),
        compiler_params=pltpu.CompilerParams(vmem_limit_bytes=16 * 2**20),
    )(tokens)


def rim_kernel(l_ref, r_ref, up, dn):
    for side, ref in enumerate((l_ref, r_ref)):
        up[side] = ref[:, 3:6]
        dn[side] = ref[:, 0:3]


def make_rims(left, right):
    vmem = pl.BlockSpec(memory_space=pltpu.VMEM)
    shape = jax.ShapeDtypeStruct((2, 12, 3, 8, 128), BF16)
    return pl.pallas_call(rim_kernel, out_shape=[shape] * 2, in_specs=[vmem] * 2, out_specs=[vmem] * 2)(left, right)


def block_kernel(own_ref, prev_ref, next_ref, l_ref, r_ref, cp_ref, cn_ref, bias0_ref, bias1_ref,
                 ga_ref, wqkv_ref, wproj_ref, gm_ref, wup_ref, wdown_ref,
                 perm_ref, left_ref, right_ref, back_ref, out_ref,
                 xs, ns, qs, kvs, os_, rs, ob, ss, ps, sems):
    def flat(v):
        return v.astype(F32).reshape(-1, C).astype(BF16)

    ones = jnp.ones((C, 128), BF16)
    gain = ga_ref[...]
    lane = lax.broadcasted_iota(jnp.int32, (SLOT, C), 1) // HD
    pad = jnp.zeros((8, C), F32)

    def both(v):
        return jnp.concatenate([v, v[:, : C - 128]], axis=1)

    def half_row(z, latw):
        levels = pl.ds(2 * z, 2)
        row = 3 * latw
        own = flat(own_ref[levels, row : row + 3])
        halo = unpack(next_ref if latw else prev_ref, 8, z)
        bias_ref = bias1_ref if latw else bias0_ref
        perm = perm_ref[...]
        own_edges = [unpack(e.at[:, row : row + 3], 8, z) for e in (l_ref, r_ref)]
        halo_edges = [unpack((cn_ref if latw else cp_ref).at[side], 8, z) for side in range(2)]
        for base, block, edges in ((0, own, own_edges), (72, halo, halo_edges)):
            got = nn(perm, block)
            edge_l = nn(left_ref[...], edges[0])
            edge_r = nn(right_ref[...], edges[1])
            for m in range(WINS):
                piece = got[72 * m : 72 * m + 72]
                if m == 0:
                    piece = piece + edge_l
                if m == WINS - 1:
                    piece = piece + edge_r
                xs[144 * m + base : 144 * m + base + 72] = piece
        for m in range(WINS):
            x = xs[144 * m : 144 * m + 144]
            mean = both(nn(x.astype(BF16), ones) * (1.0 / C))
            cen = x - mean
            var = nn((cen * cen).astype(BF16), ones) * (1.0 / C)
            inv = both(lax.rsqrt(var + EPS))
            ns[144 * m : 144 * m + 144] = (cen * inv * gain).astype(BF16)
        packed = nn(ns[...], wqkv_ref[...])
        qs[...] = packed[:, :C] * (HD ** -0.5 * LOG2E)
        kvs[...] = packed[:, C:].astype(BF16)
        def scores(c):
            m, half = unit_place(c)
            q = qs[144 * m + 32 * half : 144 * m + 32 * half + SLOT]
            rows = []
            for h in range(HEADS):
                rows.append(jnp.where(lane == h, q, 0.0))
                if h in (2, 5):
                    rows.append(pad)
            qm = jnp.concatenate(rows, axis=0).astype(BF16)
            return nt(kvs[144 * m : 144 * m + 144, :C], qm) + bias_ref[z, half]

        def soft(s):
            e = jnp.exp2(s - jnp.max(s, axis=0, keepdims=True))
            return (e * (1.0 / jnp.sum(e, axis=0, keepdims=True))).astype(BF16)

        def attend(c, p):
            m, half = unit_place(c)
            o = tn(p, kvs[144 * m : 144 * m + 144, C:])
            out = o[0:SLOT]
            for h in range(1, HEADS):
                out = jnp.where(lane == h, o[head_row(h) : head_row(h) + SLOT], out)
            os_[SLOT * c : SLOT * c + SLOT] = out
            rs[SLOT * c : SLOT * c + SLOT] = xs[144 * m + 32 * half : 144 * m + 32 * half + SLOT]

        for c in range(UNITS):
            ss[c] = scores(c)
        for c in range(UNITS):
            ps[c] = soft(ss[c])
        for c in range(UNITS):
            attend(c, ps[c])
        resid = rs[...] + nn(os_[...].astype(BF16), wproj_ref[...])
        mean = jnp.mean(resid, axis=1, keepdims=True)
        cen = resid - mean
        var = nn((cen * cen).astype(BF16), ones) * (1.0 / C)
        normed = (cen * both(lax.rsqrt(var + EPS)) * gm_ref[...]).astype(BF16)
        u = nn(normed, wup_ref[...])
        w = jnp.minimum(u * u, 25.0)
        poly = jnp.full_like(w, GELU[-1])
        for coef in GELU[-2::-1]:
            poly = poly * w + coef
        hidden = (u + u * jnp.tanh(u * poly)).astype(BF16)
        out = (resid + 0.5 * nn(hidden, wdown_ref[...])).astype(BF16)
        ob[z, :, row : row + 3] = nn(back_ref[...], out).reshape(2, 3, COLS, C).astype(BF16)

    def leave(z):
        return pltpu.make_async_copy(ob.at[z], out_ref.at[pl.ds(2 * z, 2)], sems.at[z])

    def step(z, _):
        for latw in range(2):
            half_row(z, latw)
        leave(z).start()
        return 0

    lax.fori_loop(0, ZW, step, 0)
    for z in range(ZW):
        leave(z).wait()


def run_block(tokens, halos, edges, biases, weights, maps):
    vmem = pl.BlockSpec(memory_space=pltpu.VMEM)
    operands = (tokens, *halos, *edges, *biases, *weights, *maps)
    return pl.pallas_call(
        block_kernel,
        out_shape=jax.ShapeDtypeStruct(tokens.shape, BF16),
        in_specs=[vmem] * len(operands),
        out_specs=pl.BlockSpec(memory_space=pl.ANY),
        scratch_shapes=[
            pltpu.VMEM((1008, C), F32),
            pltpu.VMEM((1008, C), BF16),
            pltpu.VMEM((1008, C), F32),
            pltpu.VMEM((1008, 2 * C), BF16),
            pltpu.VMEM((480, C), F32),
            pltpu.VMEM((480, C), F32),
            pltpu.VMEM((ZW, 2, 6, COLS, C), BF16),
            pltpu.VMEM((UNITS, 144, 256), F32),
            pltpu.VMEM((UNITS, 144, 256), BF16),
            pltpu.SemaphoreType.DMA((ZW,)),
        ],
        compiler_params=pltpu.CompilerParams(vmem_limit_bytes=24 * 2**20),
        cost_estimate=pl.CostEstimate(flops=30 * 10**9, bytes_accessed=2 * 10**6, transcendentals=0),
    )(*operands)


def passed_along(block, lat, lon):
    nlat, nlon = lax.axis_size("lat"), lax.axis_size("lon")
    route = [
        (((i - lat) % nlat) * nlon + (j - lon) % nlon, i * nlon + j) for i in range(nlat) for j in range(nlon)
    ]
    return lax.ppermute(block, ("lat", "lon"), route)


def shards(tokens, bias_table, index_table, gain_attn, w_qkv, w_proj, gain_mlp, w_up, w_down):
    place = lax.axis_index("lat")
    last = lax.axis_size("lat") - 1
    up, dn, er, el = make_packs(tokens)
    prev_table = passed_along(bias_table.reshape(-1, 128), 1, 0).reshape(bias_table.shape)
    halos = (passed_along(up, 1, 0), passed_along(dn, -1, 0))
    left, right = passed_along(er, 0, 1), passed_along(el, 0, -1)
    rim_up, rim_dn = make_rims(left, right)
    edges = (left, right, passed_along(rim_up, 1, 0), passed_along(rim_dn, -1, 0))
    keys, lanes = index_maps()
    maps = gather_maps()
    cut1 = (place == last).astype(jnp.int32).reshape(1)
    cut0 = (place == 0).astype(jnp.int32).reshape(1)
    bias1 = make_bias(cut1, bias_table, index_table, keys[1], lanes[1])
    bias0 = make_bias(cut0, prev_table, index_table, keys[0], lanes[0])
    weights = (gain_attn.reshape(1, C), w_qkv, w_proj, gain_mlp.reshape(1, C), w_up, w_down)
    return run_block(tokens, halos, edges, (bias0, bias1), weights, maps)


def solution(mesh):
    return jax.shard_map(
        shards,
        mesh=mesh,
        in_specs=(
            P(None, "lat", "lon", None),
            P("lat", None, None, None),
            P(),
            P(),
            P(),
            P(),
            P(),
            P(),
            P(),
        ),
        out_specs=P(None, "lat", "lon", None),
        check_vma=False,
    )
```

```python
import jax
import jax.numpy as jnp
import numpy as np
from jax import lax
from jax.experimental import pallas as pl
from jax.experimental.pallas import tpu as pltpu
from jax.sharding import PartitionSpec as P

HEADS = 6
HD = 32
C = 192
FFH = 768
ZW = 4
COLS = 72
UNITS = 12
WINS = 7
SLOT = 40
ROWS = 1008
NEG = -1e30
LOG2E = 1.4426950408889634
EPS = 1e-05
F32 = jnp.float32
BF16 = jnp.bfloat16
GELU = (0.7978697125591424, 0.036392285416293954, -8.782600959854813e-05, -3.66935623623972e-05, 1.4250130824069052e-06)


def head_row(h):
    return h * SLOT + (8 if h >= 3 else 0)


def unit_place(c):
    return (c + 1) // 2, (c + 1) % 2


def gather_maps():
    perm = np.zeros((504, 432), np.float32)
    left = np.zeros((72, 48), np.float32)
    right = np.zeros((72, 48), np.float32)
    back = np.zeros((440, 480), np.float32)
    for c in range(-1, 13):
        m, half = unit_place(c)
        for r in range(6):
            for j in range(6):
                row = 72 * m + 36 * half + r * 6 + j
                if c == -1:
                    left[row, r * 8 + 2 + j] = 1
                elif c == 12:
                    right[row - 432, r * 8 + j] = 1
                else:
                    perm[row, r * COLS + 6 * c + j] = 1
                    back[r * COLS + 6 * c + j, c * SLOT + 4 * half + r * 6 + j] = 1
    return [x.astype(jnp.bfloat16) for x in (perm, left, right, back)]


def place_of(rest, half, upper):
    dz = (rest >= 18).astype(jnp.int32)
    rest = rest - 18 * dz
    di = (rest >= 6).astype(jnp.int32) + (rest >= 12).astype(jnp.int32)
    return (6 * dz + 3 * upper + di) * 12 + 6 * half + rest - 6 * di


def one_hot(mask):
    return jnp.where(mask, 1.0, 0.0).astype(BF16)


def key_map(latw, third):
    rest = lax.broadcasted_iota(jnp.int32, (48, 144), 0) + 48 * third
    halo = (rest >= 72).astype(jnp.int32)
    rest = rest - 72 * halo
    half = (rest >= 36).astype(jnp.int32)
    upper = halo if latw else 1 - halo
    return one_hot(lax.broadcasted_iota(jnp.int32, (48, 144), 1) == place_of(rest - 36 * half, half, upper))


def lane_map(latw, half, third):
    slot = lax.broadcasted_iota(jnp.int32, (144, 128), 1) - (SLOT * third + 4 * half)
    place = place_of(slot, half, 1 - latw)
    mine = (slot >= 0) & (slot < 36) & (lax.broadcasted_iota(jnp.int32, (144, 128), 0) == place)
    return one_hot(mine)


def nt(a, b):
    return lax.dot_general(a, b, (((1,), (1,)), ((), ())), preferred_element_type=F32)


def tn(a, b):
    return lax.dot_general(a, b, (((0,), (0,)), ((), ())), preferred_element_type=F32)


def nn(a, b):
    return jnp.dot(a, b, preferred_element_type=F32)


POS = 3312
CH = 13


def bias_kernel(cut_ref, table1_ref, table0_ref, index_ref, out_ref, ts, lo_s, hi_s, g_s):
    for latw, table_ref in enumerate((table0_ref, table1_ref)):
        for ch in range(CH):
            width = min(256, POS - 256 * ch)
            rows = jnp.concatenate([table_ref[0, h, :, 256 * ch : 256 * ch + width] for h in range(HEADS)], axis=0)
            if width < 256:
                rows = jnp.concatenate([rows, jnp.zeros((24, 256 - width), F32)], axis=1)
            rows = rows * LOG2E
            top = rows.astype(BF16).astype(F32)
            ts[latw, 24 * ch : 24 * ch + 24] = top
            ts[latw, 24 * (CH + ch) : 24 * (CH + ch) + 24] = rows - top
    index = index_ref[...]
    index_lo = (index & 255).astype(F32).astype(BF16)
    index_hi = (index >> 8).astype(F32).astype(BF16)
    for latw in range(2):
        maps = [[lane_map(latw, half, third) for third in range(3)] for half in range(2)]
        keys = [key_map(latw, third) for third in range(3)]
        for part, dst in ((index_lo, lo_s), (index_hi, hi_s)):
            rows = [nt(keys[third], part).astype(BF16) for third in range(3)]
            for half in range(2):
                total = nn(rows[0], maps[half][0])
                for third in range(1, 3):
                    total = total + nn(rows[third], maps[half][third])
                dst[latw, 48 * half : 48 * half + 48] = total
    spread = lax.broadcasted_iota(jnp.int32, (256, 128), 0).astype(F32).astype(BF16)
    for latw in range(2):
        both = ts[latw].astype(BF16)

        def step(i, _):
            los = [lo_s[latw, pl.ds(i + 48 * half, 1), :].astype(BF16) for half in range(2)]
            his = jnp.concatenate([hi_s[latw, pl.ds(i + 48 * half, 1), :] for half in range(2)], axis=1)
            hot = jnp.concatenate([jnp.where(spread == v, BF16(1), BF16(0)) for v in los], axis=1)
            vals = nn(both, hot)
            vals = vals[: 24 * CH] + vals[24 * CH :]
            his = jnp.broadcast_to(his, (24, 256))
            acc = vals[0:24]
            for ch in range(1, CH):
                acc = jnp.where(his == float(ch), vals[24 * ch : 24 * ch + 24], acc)
            g_s[latw, i] = acc
            return 0

        lax.fori_loop(0, 48, step, 0, unroll=True)
    lane = lax.broadcasted_iota(jnp.int32, (8, 128), 1)
    for latw in range(2):
        cut = cut_ref[latw] == 1
        for z in range(ZW):
            for half in range(2):
                for tile in range(2):
                    for k8 in range(6):
                        three = [
                            g_s[latw, 8 * k8 : 8 * k8 + 8, (3 * tile + h) * ZW + z, 128 * half : 128 * half + 128]
                            for h in range(3)
                        ]
                        for third in range(3):
                            moved = [
                                three[h] if h == third else pltpu.roll(three[h], (SLOT * (h - third)) % 128, 1)
                                for h in range(3)
                            ]
                            got = jnp.where(lane < SLOT, moved[0], jnp.where(lane < 2 * SLOT, moved[1], moved[2]))
                            row = 48 * third + 8 * k8
                            if row >= 72:
                                got = jnp.where(cut, NEG, got)
                            out_ref[latw, z, half, row : row + 8, 128 * tile : 128 * tile + 128] = got


def make_bias(cut, table1, table0, index_table):
    return pl.pallas_call(
        bias_kernel,
        out_shape=jax.ShapeDtypeStruct((2, ZW, 2, 144, 256), F32),
        in_specs=[pl.BlockSpec(memory_space=pltpu.SMEM)] + [pl.BlockSpec(memory_space=pltpu.VMEM)] * 3,
        out_specs=pl.BlockSpec(memory_space=pltpu.VMEM),
        scratch_shapes=[
            pltpu.VMEM((2, 48 * CH, 256), F32),
            pltpu.VMEM((2, 96, 128), F32),
            pltpu.VMEM((2, 96, 128), F32),
            pltpu.VMEM((2, 48, 24, 256), F32),
        ],
        compiler_params=pltpu.CompilerParams(vmem_limit_bytes=16 * 2**20),
        cost_estimate=pl.CostEstimate(flops=14 * 10**9, bytes_accessed=2 * 10**6, transcendentals=0),
    )(cut, table1, table0, index_table)


def packed_shape(levels, rows, cols):
    return jax.ShapeDtypeStruct((3 * levels // 2, rows, cols, 128), BF16)


def pack(dst, x):
    levels = x.shape[0]
    dst[:levels] = x[..., :128]
    for i in range(levels // 2):
        dst[levels + i] = jnp.concatenate([x[2 * i, ..., 128:], x[2 * i + 1, ..., 128:]], axis=-1)


def unpack(src, levels, z):
    low = src[pl.ds(2 * z, 2)].astype(F32)
    high = src[pl.ds(levels + z, 1)].astype(F32)
    rows = low.shape[1] * low.shape[2]
    low = low.reshape(2, rows, 128)
    high = high.reshape(rows, 128)
    parts = [jnp.concatenate([low[dz], high[:, 64 * dz : 64 * dz + 64]], axis=1) for dz in range(2)]
    return jnp.concatenate(parts, axis=0).astype(BF16)


def pack_kernel(x_ref, up, dn, er, el):
    pack(up, x_ref[:, 3:6])
    pack(dn, x_ref[:, 0:3])
    pack(er, x_ref[:, :, COLS - 8 :])
    pack(el, x_ref[:, :, :8])


def make_packs(tokens):
    vmem = pl.BlockSpec(memory_space=pltpu.VMEM)
    shapes = [packed_shape(8, 3, COLS)] * 2 + [packed_shape(8, 6, 8)] * 2
    return pl.pallas_call(
        pack_kernel,
        out_shape=shapes,
        in_specs=[vmem],
        out_specs=[vmem] * len(shapes),
        compiler_params=pltpu.CompilerParams(vmem_limit_bytes=16 * 2**20),
    )(tokens)


def rim_kernel(l_ref, r_ref, up, dn):
    for side, ref in enumerate((l_ref, r_ref)):
        up[side] = ref[:, 3:6]
        dn[side] = ref[:, 0:3]


def make_rims(left, right):
    vmem = pl.BlockSpec(memory_space=pltpu.VMEM)
    shape = jax.ShapeDtypeStruct((2, 12, 3, 8, 128), BF16)
    return pl.pallas_call(rim_kernel, out_shape=[shape] * 2, in_specs=[vmem] * 2, out_specs=[vmem] * 2,
                          compiler_params=pltpu.CompilerParams(vmem_limit_bytes=8 * 2**20))(left, right)


def block_kernel(own_ref, prev_ref, next_ref, l_ref, r_ref, cp_ref, cn_ref, bias_ref,
                 ga_ref, wqkv_ref, wproj_ref, gm_ref, wup_ref, wdown_ref,
                 perm_ref, left_ref, right_ref, back_ref, out_ref,
                 xs, ns, qs, kvs, os_, rs, ob, ss, ps, sems):
    def flat(v):
        return v.astype(F32).reshape(-1, C).astype(BF16)

    ones = jnp.ones((C, 128), BF16)
    gain = ga_ref[...]
    lane = lax.broadcasted_iota(jnp.int32, (SLOT, C), 1) // HD
    pad = jnp.zeros((8, C), F32)

    def both(v):
        return jnp.concatenate([v, v[:, : C - 128]], axis=1)

    halves = [(latw, c) for latw in range(2) for c in range(UNITS)]

    def gather(z, latw):
        levels = pl.ds(2 * z, 2)
        row = 3 * latw
        own = flat(own_ref[levels, row : row + 3])
        halo = unpack(next_ref if latw else prev_ref, 8, z)
        perm = perm_ref[...]
        own_edges = [unpack(e.at[:, row : row + 3], 8, z) for e in (l_ref, r_ref)]
        halo_edges = [unpack((cn_ref if latw else cp_ref).at[side], 8, z) for side in range(2)]
        for base, block, edges in ((0, own, own_edges), (72, halo, halo_edges)):
            got = nn(perm, block)
            edge_l = nn(left_ref[...], edges[0])
            edge_r = nn(right_ref[...], edges[1])
            for m in range(WINS):
                piece = got[72 * m : 72 * m + 72]
                if m == 0:
                    piece = piece + edge_l
                if m == WINS - 1:
                    piece = piece + edge_r
                first = ROWS * latw + 144 * m + base
                xs[first : first + 72] = piece

    def first_norm(r0):
        x = xs[r0 : r0 + 144]
        mean = both(nn(x.astype(BF16), ones) * (1.0 / C))
        cen = x - mean
        var = nn((cen * cen).astype(BF16), ones) * (1.0 / C)
        inv = both(lax.rsqrt(var + EPS))
        ns[r0 : r0 + 144] = (cen * inv * gain).astype(BF16)

    def scores(z, latw, c):
        m, half = unit_place(c)
        r0 = ROWS * latw + 144 * m
        q = qs[r0 + 32 * half : r0 + 32 * half + SLOT]
        rows = []
        for h in range(HEADS):
            rows.append(jnp.where(lane == h, q, 0.0))
            if h in (2, 5):
                rows.append(pad)
        qm = jnp.concatenate(rows, axis=0).astype(BF16)
        return nt(kvs[r0 : r0 + 144, :C], qm) + bias_ref[latw, z, half]

    def soft(s):
        e = jnp.exp2(s - jnp.max(s, axis=0, keepdims=True))
        return (e * (1.0 / jnp.sum(e, axis=0, keepdims=True))).astype(BF16)

    def attend(latw, c, p):
        m, half = unit_place(c)
        r0 = ROWS * latw + 144 * m
        o = tn(p, kvs[r0 : r0 + 144, C:])
        out = o[0:SLOT]
        for h in range(1, HEADS):
            out = jnp.where(lane == h, o[head_row(h) : head_row(h) + SLOT], out)
        to = SLOT * (UNITS * latw + c)
        os_[to : to + SLOT] = out
        rs[to : to + SLOT] = xs[r0 + 32 * half : r0 + 32 * half + SLOT]

    def level_pair(z):
        for latw in range(2):
            gather(z, latw)
        for r0 in range(0, 2 * ROWS, 144):
            first_norm(r0)
        packed = nn(ns[...], wqkv_ref[...])
        qs[...] = packed[:, :C] * (HD ** -0.5 * LOG2E)
        kvs[...] = packed[:, C:].astype(BF16)
        for n, (latw, c) in enumerate(halves):
            ss[n] = scores(z, latw, c)
        for n in range(2 * UNITS):
            ps[n] = soft(ss[n])
        for n, (latw, c) in enumerate(halves):
            attend(latw, c, ps[n])
        resid = rs[...] + nn(os_[...].astype(BF16), wproj_ref[...])
        mean = jnp.mean(resid, axis=1, keepdims=True)
        cen = resid - mean
        var = nn((cen * cen).astype(BF16), ones) * (1.0 / C)
        normed = (cen * both(lax.rsqrt(var + EPS)) * gm_ref[...]).astype(BF16)
        u = nn(normed, wup_ref[...])
        w = u * u
        poly = w * GELU[-1] + GELU[-2]
        for coef in GELU[-3::-1]:
            poly = poly * w + coef
        hidden = (u + u * jnp.tanh(u * poly)).astype(BF16)
        out = (resid + 0.5 * nt(hidden, wdown_ref[...])).astype(BF16)
        for latw in range(2):
            got = nn(back_ref[:432], out[SLOT * UNITS * latw : SLOT * UNITS * (latw + 1)])
            ob[z, :, 3 * latw : 3 * latw + 3] = got.reshape(2, 3, COLS, C).astype(BF16)

    def leave(z):
        return pltpu.make_async_copy(ob.at[z], out_ref.at[pl.ds(2 * z, 2)], sems.at[z])

    def step(z, _):
        level_pair(z)
        leave(z).start()
        return 0

    lax.fori_loop(0, ZW, step, 0)
    for z in range(ZW):
        leave(z).wait()


def run_block(tokens, halos, edges, bias, weights, maps):
    vmem = pl.BlockSpec(memory_space=pltpu.VMEM)
    operands = (tokens, *halos, *edges, bias, *weights, *maps)
    return pl.pallas_call(
        block_kernel,
        out_shape=jax.ShapeDtypeStruct(tokens.shape, BF16),
        in_specs=[vmem] * len(operands),
        out_specs=pl.BlockSpec(memory_space=pl.ANY),
        scratch_shapes=[
            pltpu.VMEM((2 * ROWS, C), F32),
            pltpu.VMEM((2 * ROWS, C), BF16),
            pltpu.VMEM((2 * ROWS, C), F32),
            pltpu.VMEM((2 * ROWS, 2 * C), BF16),
            pltpu.VMEM((2 * SLOT * UNITS, C), F32),
            pltpu.VMEM((2 * SLOT * UNITS, C), F32),
            pltpu.VMEM((ZW, 2, 6, COLS, C), BF16),
            pltpu.VMEM((2 * UNITS, 144, 256), F32),
            pltpu.VMEM((2 * UNITS, 144, 256), BF16),
            pltpu.SemaphoreType.DMA((ZW,)),
        ],
        compiler_params=pltpu.CompilerParams(vmem_limit_bytes=36 * 2**20),
        cost_estimate=pl.CostEstimate(flops=30 * 10**9, bytes_accessed=2 * 10**6, transcendentals=0),
    )(*operands)


def passed_along(block, lat, lon):
    nlat, nlon = lax.axis_size("lat"), lax.axis_size("lon")
    route = [
        (((i - lat) % nlat) * nlon + (j - lon) % nlon, i * nlon + j) for i in range(nlat) for j in range(nlon)
    ]
    return lax.ppermute(block, ("lat", "lon"), route)


def shards(tokens, bias_table, index_table, gain_attn, w_qkv, w_proj, gain_mlp, w_up, w_down):
    place = lax.axis_index("lat")
    last = lax.axis_size("lat") - 1
    up, dn, er, el = make_packs(tokens)
    table = bias_table.transpose(0, 2, 1, 3)
    prev_table = passed_along(table, 1, 0)
    halos = (passed_along(up, 1, 0), passed_along(dn, -1, 0))
    left, right = passed_along(er, 0, 1), passed_along(el, 0, -1)
    rim_up, rim_dn = make_rims(left, right)
    edges = (left, right, passed_along(rim_up, 1, 0), passed_along(rim_dn, -1, 0))
    maps = gather_maps()
    cut = jnp.stack([place == 0, place == last]).astype(jnp.int32)
    bias = make_bias(cut, table, prev_table, index_table)
    weights = (gain_attn.reshape(1, C), w_qkv, w_proj, gain_mlp.reshape(1, C), w_up, w_down.T)
    return run_block(tokens, halos, edges, bias, weights, maps)


def solution(mesh):
    return jax.shard_map(
        shards,
        mesh=mesh,
        in_specs=(
            P(None, "lat", "lon", None),
            P("lat", None, None, None),
            P(),
            P(),
            P(),
            P(),
            P(),
            P(),
            P(),
        ),
        out_specs=P(None, "lat", "lon", None),
        check_vma=False,
    )
```

```python
import jax
import jax.numpy as jnp
import numpy as np
from jax import lax
from jax.experimental import pallas as pl
from jax.experimental.pallas import tpu as pltpu
from jax.sharding import PartitionSpec as P

HEADS = 6
HD = 32
C = 192
FFH = 768
ZW = 4
COLS = 72
UNITS = 12
WINS = 7
SLOT = 40
ROWS = 1008
NEG = -1e30
LOG2E = 1.4426950408889634
EPS = 1e-05
F32 = jnp.float32
BF16 = jnp.bfloat16
GELU = (0.7978697125591424, 0.036392285416293954, -8.782600959854813e-05, -3.66935623623972e-05, 1.4250130824069052e-06)


def head_row(h):
    return h * SLOT + (8 if h >= 3 else 0)


def unit_place(c):
    return (c + 1) // 2, (c + 1) % 2


def gather_maps():
    perm = np.zeros((504, 432), np.float32)
    left = np.zeros((72, 48), np.float32)
    right = np.zeros((72, 48), np.float32)
    back = np.zeros((440, 480), np.float32)
    for c in range(-1, 13):
        m, half = unit_place(c)
        for r in range(6):
            for j in range(6):
                row = 72 * m + 36 * half + r * 6 + j
                if c == -1:
                    left[row, r * 8 + 2 + j] = 1
                elif c == 12:
                    right[row - 432, r * 8 + j] = 1
                else:
                    perm[row, r * COLS + 6 * c + j] = 1
                    back[r * COLS + 6 * c + j, c * SLOT + 4 * half + r * 6 + j] = 1
    return [x.astype(jnp.bfloat16) for x in (perm, left, right, back)]


def place_of(rest, half, upper):
    dz = (rest >= 18).astype(jnp.int32)
    rest = rest - 18 * dz
    di = (rest >= 6).astype(jnp.int32) + (rest >= 12).astype(jnp.int32)
    return (6 * dz + 3 * upper + di) * 12 + 6 * half + rest - 6 * di


def one_hot(mask):
    return jnp.where(mask, 1.0, 0.0).astype(BF16)


def key_map(latw, third):
    rest = lax.broadcasted_iota(jnp.int32, (48, 144), 0) + 48 * third
    halo = (rest >= 72).astype(jnp.int32)
    rest = rest - 72 * halo
    half = (rest >= 36).astype(jnp.int32)
    upper = halo if latw else 1 - halo
    return one_hot(lax.broadcasted_iota(jnp.int32, (48, 144), 1) == place_of(rest - 36 * half, half, upper))


def lane_map(latw, half, third):
    slot = lax.broadcasted_iota(jnp.int32, (144, 128), 1) - (SLOT * third + 4 * half)
    place = place_of(slot, half, 1 - latw)
    mine = (slot >= 0) & (slot < 36) & (lax.broadcasted_iota(jnp.int32, (144, 128), 0) == place)
    return one_hot(mine)


def nt(a, b):
    return lax.dot_general(a, b, (((1,), (1,)), ((), ())), preferred_element_type=F32)


def tn(a, b):
    return lax.dot_general(a, b, (((0,), (0,)), ((), ())), preferred_element_type=F32)


def nn(a, b):
    return jnp.dot(a, b, preferred_element_type=F32)


POS = 3312
CH = 13


def bias_kernel(cut_ref, table1_ref, table0_ref, index_ref, out_ref, ts, lo_s, hi_s, g_s):
    for latw, table_ref in enumerate((table0_ref, table1_ref)):
        for ch in range(CH):
            width = min(256, POS - 256 * ch)
            rows = jnp.concatenate([table_ref[0, h, :, 256 * ch : 256 * ch + width] for h in range(HEADS)], axis=0)
            if width < 256:
                rows = jnp.concatenate([rows, jnp.zeros((24, 256 - width), F32)], axis=1)
            rows = rows * LOG2E
            top = rows.astype(BF16).astype(F32)
            ts[latw, 24 * ch : 24 * ch + 24] = top
            ts[latw, 24 * (CH + ch) : 24 * (CH + ch) + 24] = rows - top
    index = index_ref[...]
    index_lo = (index & 255).astype(F32).astype(BF16)
    index_hi = (index >> 8).astype(F32).astype(BF16)
    for latw in range(2):
        maps = [[lane_map(latw, half, third) for third in range(3)] for half in range(2)]
        keys = [key_map(latw, third) for third in range(3)]
        for part, dst in ((index_lo, lo_s), (index_hi, hi_s)):
            rows = [nt(keys[third], part).astype(BF16) for third in range(3)]
            for half in range(2):
                total = nn(rows[0], maps[half][0])
                for third in range(1, 3):
                    total = total + nn(rows[third], maps[half][third])
                dst[latw, 48 * half : 48 * half + 48] = total
    spread = lax.broadcasted_iota(jnp.int32, (256, 128), 0).astype(F32).astype(BF16)
    for latw in range(2):
        both = ts[latw].astype(BF16)

        def step(i, _):
            los = [lo_s[latw, pl.ds(i + 48 * half, 1), :].astype(BF16) for half in range(2)]
            his = jnp.concatenate([hi_s[latw, pl.ds(i + 48 * half, 1), :] for half in range(2)], axis=1)
            hot = jnp.concatenate([jnp.where(spread == v, BF16(1), BF16(0)) for v in los], axis=1)
            vals = nn(both, hot)
            vals = vals[: 24 * CH] + vals[24 * CH :]
            his = jnp.broadcast_to(his, (24, 256))
            acc = vals[0:24]
            for ch in range(1, CH):
                acc = jnp.where(his == float(ch), vals[24 * ch : 24 * ch + 24], acc)
            g_s[latw, i] = acc
            return 0

        lax.fori_loop(0, 48, step, 0, unroll=True)
    lane = lax.broadcasted_iota(jnp.int32, (8, 128), 1)
    for latw in range(2):
        cut = cut_ref[latw] == 1
        for z in range(ZW):
            for half in range(2):
                for tile in range(2):
                    for k8 in range(6):
                        three = [
                            g_s[latw, 8 * k8 : 8 * k8 + 8, (3 * tile + h) * ZW + z, 128 * half : 128 * half + 128]
                            for h in range(3)
                        ]
                        for third in range(3):
                            moved = [
                                three[h] if h == third else pltpu.roll(three[h], (SLOT * (h - third)) % 128, 1)
                                for h in range(3)
                            ]
                            got = jnp.where(lane < SLOT, moved[0], jnp.where(lane < 2 * SLOT, moved[1], moved[2]))
                            row = 48 * third + 8 * k8
                            if row >= 72:
                                got = jnp.where(cut, NEG, got)
                            out_ref[latw, z, half, row : row + 8, 128 * tile : 128 * tile + 128] = got


def make_bias(cut, table1, table0, index_table):
    return pl.pallas_call(
        bias_kernel,
        out_shape=jax.ShapeDtypeStruct((2, ZW, 2, 144, 256), F32),
        in_specs=[pl.BlockSpec(memory_space=pltpu.SMEM)] + [pl.BlockSpec(memory_space=pltpu.VMEM)] * 3,
        out_specs=pl.BlockSpec(memory_space=pltpu.VMEM),
        scratch_shapes=[
            pltpu.VMEM((2, 48 * CH, 256), F32),
            pltpu.VMEM((2, 96, 128), F32),
            pltpu.VMEM((2, 96, 128), F32),
            pltpu.VMEM((2, 48, 24, 256), F32),
        ],
        compiler_params=pltpu.CompilerParams(vmem_limit_bytes=16 * 2**20),
        cost_estimate=pl.CostEstimate(flops=14 * 10**9, bytes_accessed=2 * 10**6, transcendentals=0),
    )(cut, table1, table0, index_table)


def packed_shape(levels, rows, cols):
    return jax.ShapeDtypeStruct((3 * levels // 2, rows, cols, 128), BF16)


def pack(dst, x):
    levels = x.shape[0]
    dst[:levels] = x[..., :128]
    for i in range(levels // 2):
        dst[levels + i] = jnp.concatenate([x[2 * i, ..., 128:], x[2 * i + 1, ..., 128:]], axis=-1)


def unpack(src, levels, z):
    low = src[pl.ds(2 * z, 2)].astype(F32)
    high = src[pl.ds(levels + z, 1)].astype(F32)
    rows = low.shape[1] * low.shape[2]
    low = low.reshape(2, rows, 128)
    high = high.reshape(rows, 128)
    parts = [jnp.concatenate([low[dz], high[:, 64 * dz : 64 * dz + 64]], axis=1) for dz in range(2)]
    return jnp.concatenate(parts, axis=0).astype(BF16)


def pack_kernel(x_ref, up, dn, er, el):
    pack(up, x_ref[:, 3:6])
    pack(dn, x_ref[:, 0:3])
    pack(er, x_ref[:, :, COLS - 8 :])
    pack(el, x_ref[:, :, :8])


def make_packs(tokens):
    vmem = pl.BlockSpec(memory_space=pltpu.VMEM)
    shapes = [packed_shape(8, 3, COLS)] * 2 + [packed_shape(8, 6, 8)] * 2
    return pl.pallas_call(
        pack_kernel,
        out_shape=shapes,
        in_specs=[vmem],
        out_specs=[vmem] * len(shapes),
        compiler_params=pltpu.CompilerParams(vmem_limit_bytes=16 * 2**20),
    )(tokens)


def rim_kernel(l_ref, r_ref, up, dn):
    for side, ref in enumerate((l_ref, r_ref)):
        up[side] = ref[:, 3:6]
        dn[side] = ref[:, 0:3]


def make_rims(left, right):
    vmem = pl.BlockSpec(memory_space=pltpu.VMEM)
    shape = jax.ShapeDtypeStruct((2, 12, 3, 8, 128), BF16)
    return pl.pallas_call(rim_kernel, out_shape=[shape] * 2, in_specs=[vmem] * 2, out_specs=[vmem] * 2,
                          compiler_params=pltpu.CompilerParams(vmem_limit_bytes=8 * 2**20))(left, right)


def block_kernel(own_ref, prev_ref, next_ref, l_ref, r_ref, cp_ref, cn_ref, bias_ref,
                 ga_ref, wqkv_ref, wproj_ref, gm_ref, wup_ref, wdown_ref,
                 perm_ref, left_ref, right_ref, back_ref, out_ref,
                 xs, ns, qs, kvs, os_, rs, ob, ss, ps, sems):
    def flat(v):
        return v.astype(F32).reshape(-1, C).astype(BF16)

    ones = jnp.ones((C, 128), BF16)
    gain = ga_ref[...]
    lane = lax.broadcasted_iota(jnp.int32, (SLOT, C), 1) // HD
    pad = jnp.zeros((8, C), F32)

    def both(v):
        return jnp.concatenate([v, v[:, : C - 128]], axis=1)

    halves = [(latw, c) for latw in range(2) for c in range(UNITS)]
    groups = [(latw, [c for c in (2 * m - 1, 2 * m) if 0 <= c < UNITS]) for latw in range(2) for m in range(WINS)]

    def gather(z, latw):
        levels = pl.ds(2 * z, 2)
        row = 3 * latw
        own = flat(own_ref[levels, row : row + 3])
        halo = unpack(next_ref if latw else prev_ref, 8, z)
        perm = perm_ref[...]
        own_edges = [unpack(e.at[:, row : row + 3], 8, z) for e in (l_ref, r_ref)]
        halo_edges = [unpack((cn_ref if latw else cp_ref).at[side], 8, z) for side in range(2)]
        for base, block, edges in ((0, own, own_edges), (72, halo, halo_edges)):
            got = nn(perm, block)
            edge_l = nn(left_ref[...], edges[0])
            edge_r = nn(right_ref[...], edges[1])
            for m in range(WINS):
                piece = got[72 * m : 72 * m + 72]
                if m == 0:
                    piece = piece + edge_l
                if m == WINS - 1:
                    piece = piece + edge_r
                first = ROWS * latw + 144 * m + base
                xs[first : first + 72] = piece

    def first_norm(r0):
        x = xs[r0 : r0 + 144]
        mean = both(nn(x.astype(BF16), ones) * (1.0 / C))
        cen = x - mean
        var = nn((cen * cen).astype(BF16), ones) * (1.0 / C)
        inv = both(lax.rsqrt(var + EPS))
        ns[r0 : r0 + 144] = (cen * inv * gain).astype(BF16)

    def scores(z, latw, c):
        m, half = unit_place(c)
        r0 = ROWS * latw + 144 * m
        q = qs[r0 + 32 * half : r0 + 32 * half + SLOT]
        rows = []
        for h in range(HEADS):
            rows.append(jnp.where(lane == h, q, 0.0))
            if h in (2, 5):
                rows.append(pad)
        qm = jnp.concatenate(rows, axis=0).astype(BF16)
        return nt(kvs[r0 : r0 + 144, :C], qm) + bias_ref[latw, z, half]

    def soft(s):
        e = jnp.exp2(s - jnp.max(s, axis=0, keepdims=True))
        return (e * (1.0 / jnp.sum(e, axis=0, keepdims=True))).astype(BF16)

    def attend(latw, units, p):
        m, half = unit_place(units[0])
        r0 = ROWS * latw + 144 * m
        both_halves = tn(p, kvs[r0 : r0 + 144, C:])
        for k, c in enumerate(units):
            o = both_halves[256 * k : 256 * k + 256]
            out = o[0:SLOT]
            for h in range(1, HEADS):
                out = jnp.where(lane == h, o[head_row(h) : head_row(h) + SLOT], out)
            m, half = unit_place(c)
            to = SLOT * (UNITS * latw + c)
            os_[to : to + SLOT] = out
            rs[to : to + SLOT] = xs[r0 + 32 * half : r0 + 32 * half + SLOT]

    def level_pair(z):
        for latw in range(2):
            gather(z, latw)
        for r0 in range(0, 2 * ROWS, 144):
            first_norm(r0)
        packed = nn(ns[...], wqkv_ref[...])
        qs[...] = packed[:, :C] * (HD ** -0.5 * LOG2E)
        kvs[...] = packed[:, C:].astype(BF16)
        for n, (latw, c) in enumerate(halves):
            ss[n] = scores(z, latw, c)
        for n in range(2 * UNITS):
            ps[n] = soft(ss[n])
        for latw, units in groups:
            k = UNITS * latw + units[0]
            attend(latw, units, ps[k] if len(units) == 1 else jnp.concatenate([ps[k], ps[k + 1]], axis=1))
        resid = rs[...] + nn(os_[...].astype(BF16), wproj_ref[...])
        mean = jnp.mean(resid, axis=1, keepdims=True)
        cen = resid - mean
        var = jnp.mean(cen * cen, axis=1, keepdims=True)
        normed = (cen * lax.rsqrt(var + EPS) * gm_ref[...]).astype(BF16)
        u = nn(normed, wup_ref[...])
        w = u * u
        poly = w * GELU[-1] + GELU[-2]
        for coef in GELU[-3::-1]:
            poly = poly * w + coef
        hidden = (u + u * jnp.tanh(u * poly)).astype(BF16)
        out = (resid + 0.5 * nt(hidden, wdown_ref[...])).astype(BF16)
        for latw in range(2):
            got = nn(back_ref[:432], out[SLOT * UNITS * latw : SLOT * UNITS * (latw + 1)])
            ob[z, :, 3 * latw : 3 * latw + 3] = got.reshape(2, 3, COLS, C).astype(BF16)

    def leave(z):
        return pltpu.make_async_copy(ob.at[z], out_ref.at[pl.ds(2 * z, 2)], sems.at[z])

    def step(z, _):
        level_pair(z)
        leave(z).start()
        return 0

    lax.fori_loop(0, ZW, step, 0)
    for z in range(ZW):
        leave(z).wait()


def run_block(tokens, halos, edges, bias, weights, maps):
    vmem = pl.BlockSpec(memory_space=pltpu.VMEM)
    operands = (tokens, *halos, *edges, bias, *weights, *maps)
    return pl.pallas_call(
        block_kernel,
        out_shape=jax.ShapeDtypeStruct(tokens.shape, BF16),
        in_specs=[vmem] * len(operands),
        out_specs=pl.BlockSpec(memory_space=pl.ANY),
        scratch_shapes=[
            pltpu.VMEM((2 * ROWS, C), F32),
            pltpu.VMEM((2 * ROWS, C), BF16),
            pltpu.VMEM((2 * ROWS, C), F32),
            pltpu.VMEM((2 * ROWS, 2 * C), BF16),
            pltpu.VMEM((2 * SLOT * UNITS, C), F32),
            pltpu.VMEM((2 * SLOT * UNITS, C), F32),
            pltpu.VMEM((ZW, 2, 6, COLS, C), BF16),
            pltpu.VMEM((2 * UNITS, 144, 256), F32),
            pltpu.VMEM((2 * UNITS, 144, 256), BF16),
            pltpu.SemaphoreType.DMA((ZW,)),
        ],
        compiler_params=pltpu.CompilerParams(vmem_limit_bytes=36 * 2**20),
        cost_estimate=pl.CostEstimate(flops=30 * 10**9, bytes_accessed=2 * 10**6, transcendentals=0),
    )(*operands)


def passed_along(block, lat, lon):
    nlat, nlon = lax.axis_size("lat"), lax.axis_size("lon")
    route = [
        (((i - lat) % nlat) * nlon + (j - lon) % nlon, i * nlon + j) for i in range(nlat) for j in range(nlon)
    ]
    return lax.ppermute(block, ("lat", "lon"), route)


def shards(tokens, bias_table, index_table, gain_attn, w_qkv, w_proj, gain_mlp, w_up, w_down):
    place = lax.axis_index("lat")
    last = lax.axis_size("lat") - 1
    up, dn, er, el = make_packs(tokens)
    table = bias_table.transpose(0, 2, 1, 3)
    prev_table = passed_along(table, 1, 0)
    halos = (passed_along(up, 1, 0), passed_along(dn, -1, 0))
    left, right = passed_along(er, 0, 1), passed_along(el, 0, -1)
    rim_up, rim_dn = make_rims(left, right)
    edges = (left, right, passed_along(rim_up, 1, 0), passed_along(rim_dn, -1, 0))
    maps = gather_maps()
    cut = jnp.stack([place == 0, place == last]).astype(jnp.int32)
    bias = make_bias(cut, table, prev_table, index_table)
    weights = (gain_attn.reshape(1, C), w_qkv, w_proj, gain_mlp.reshape(1, C), w_up, w_down.T)
    return run_block(tokens, halos, edges, bias, weights, maps)


def solution(mesh):
    return jax.shard_map(
        shards,
        mesh=mesh,
        in_specs=(
            P(None, "lat", "lon", None),
            P("lat", None, None, None),
            P(),
            P(),
            P(),
            P(),
            P(),
            P(),
            P(),
        ),
        out_specs=P(None, "lat", "lon", None),
        check_vma=False,
    )
```
